512 devices in a mesh: frame: 32 (over z, x), feat: 16 (over y, core).
Axes of the slice: x: 4, y: 8, z: 8, core: 2. Of those that a mesh axis runs over, the one named last changes fastest.
Arguments:
- trajectory: bfloat16 [24576, 24576], P('frame', 'feat'), may hold values from -40 to 40
- test_matrix: bfloat16 [24576, 512], P('feat'), may hold values from -0.0390625 to 0.0390625
Outputs:
- orthobasis: bfloat16 [24576, 512], P('frame')
- projected: bfloat16 [512, 24576], P('frame', 'feat')
- small_gram: float32 [512, 512], P('frame')
The draws below stay inside these ranges and needn't reach their ends.
All inputs are finite; a program needn't handle non-finite values.
Results may differ from the reference program's by a relative error of at most 0.015.
Values may be sent and summed in bfloat16 or wider, within the bound.
No kernel may reach another device: no remote copies, remote signals or barrier semaphores. Data moves between devices by JAX's collectives and lax.ppermute only.
A program may use at most 64 MiB of HBM per device.

```python
import math
import jax
import jax.numpy as jnp
from jax import lax

D = 24576
K = 512
FRAMES = 24576


def draw_trajectory(key, part):
    key = jax.random.fold_in(key, 7)
    key_main, key_rows, key_cols = jax.random.split(key, 3)
    position = jnp.arange(FRAMES, dtype=jnp.float32) / FRAMES
    jitter = jax.random.uniform(key_rows, (FRAMES,), jnp.float32, 0.0, 0.3)
    row_scale = jnp.power(10.0, position - 0.8 + jitter)
    col_scale = jnp.exp(jax.random.uniform(key_cols, (D,), jnp.float32, -math.log(2.0), math.log(2.0)))
    values = jnp.clip(jax.random.normal(key_main, (FRAMES, D), jnp.float32), -6.0, 6.0)
    return (values * row_scale[:, None] * col_scale[None, :]).astype(jnp.bfloat16)


def level_of(key, dims, shards, least, high):
    loudness = 1.0
    for dim, parts in shards:
        steps = jax.random.uniform(jax.random.fold_in(jax.random.fold_in(key, 6), dim), (parts,), jnp.float32, least / len(shards), high / len(shards))
        loudness = loudness * jnp.repeat(jnp.exp(steps), dims[dim] // parts).reshape((-1,) + (1,) * (len(dims) - 1 - dim))
    return loudness


def bell_draw(rng, dims, scale, most, pieces=(), kind=jnp.bfloat16):
    array = scale * jax.random.normal(rng, dims, jnp.float32)
    if pieces:
        array = array * level_of(rng, dims, pieces, -0.22, 0.18)
    return jnp.clip(array, -most, most).astype(kind)


def setup_inputs(seed: int = 0) -> dict:
    seeds = jax.random.split(jax.random.key(seed), 3)
    trajectory = draw_trajectory(jax.random.fold_in(seeds[2], 71), 0)
    test_matrix = bell_draw(seeds[1], (D, K), D ** -0.5, 0.0390625, ((0, 16),))
    return dict(trajectory=trajectory, test_matrix=test_matrix)


def reference(trajectory, test_matrix):
    sketch = jnp.dot(trajectory.astype(jnp.float32), test_matrix.astype(jnp.float32), preferred_element_type=jnp.float32)
    gram = jnp.dot(sketch.T, sketch, precision=lax.Precision.HIGHEST) / FRAMES
    factor = jnp.linalg.cholesky(gram)
    solved = jax.scipy.linalg.solve_triangular(factor, sketch.T, lower=True)
    orthobasis = solved.T.astype(jnp.bfloat16)
    summed = jnp.dot(orthobasis.T.astype(jnp.float32), trajectory.astype(jnp.float32), preferred_element_type=jnp.float32)
    projected = (summed / math.sqrt(FRAMES)).astype(jnp.bfloat16)
    small_gram = jnp.dot(projected.astype(jnp.float32), projected.T.astype(jnp.float32), preferred_element_type=jnp.float32) / D
    return (orthobasis, projected, small_gram)
```

```python
import math

import jax
import jax.numpy as jnp
from jax import lax
from jax.sharding import PartitionSpec as P


def lines(axis_size, stride):
    return [list(range(s, axis_size, stride)) for s in range(stride)]


def scatter_sum(blocks, axis, groups=None):
    got = lax.all_to_all(blocks, axis, 0, 0, axis_index_groups=groups)
    return jnp.sum(got.astype(jnp.float32), axis=0)


def gather(block, axis, count, groups=None):
    copies = jnp.broadcast_to(block, (count,) + block.shape)
    return lax.all_to_all(copies, axis, 0, 0, axis_index_groups=groups)


def swap_cores(block):
    count = lax.axis_size("feat")
    return lax.ppermute(block, "feat", [(i, i ^ 1) for i in range(count)])


def feat_scatter_sum(whole):
    count = lax.axis_size("feat")
    core = lax.axis_index("feat") % 2
    rows, columns = whole.shape
    halves = whole.reshape(2, rows // 2, columns)
    keep = lax.dynamic_index_in_dim(halves, core, 0, keepdims=False)
    give = lax.dynamic_index_in_dim(halves, 1 - core, 0, keepdims=False)
    half = keep + swap_cores(give)
    return scatter_sum(half.reshape(count // 2, -1, columns), "feat", lines(count, 2))


def feat_gather(block):
    count = lax.axis_size("feat")
    core = lax.axis_index("feat") % 2
    half = gather(block, "feat", count // 2, lines(count, 2)).reshape(-1, block.shape[1])
    other = swap_cores(half)
    low = jnp.where(core == 0, half, other)
    high = jnp.where(core == 0, other, half)
    return jnp.concatenate([low, high], axis=0)


def to_basis(sketch, gram):
    factor = jnp.linalg.cholesky(gram)
    solved = jax.scipy.linalg.solve_triangular(factor, sketch.T, lower=True)
    return solved.T.astype(jnp.bfloat16)


def per_device(trajectory, test_matrix):
    frame_count = lax.axis_size("frame")
    feat_count = lax.axis_size("feat")
    local_rows, local_feats = trajectory.shape
    frames_all = local_rows * frame_count
    features_all = local_feats * feat_count
    rank = test_matrix.shape[1]

    partial_sketch = jnp.dot(trajectory, test_matrix, preferred_element_type=jnp.float32)
    sketch = feat_gather(feat_scatter_sum(partial_sketch))

    width = rank // feat_count
    place = lax.axis_index("feat") % 2 * (feat_count // 2) + lax.axis_index("feat") // 2
    columns = lax.dynamic_slice_in_dim(sketch, place * width, width, axis=1)
    gram_rows = jnp.dot(columns.T, sketch, precision=lax.Precision.HIGHEST) / frames_all
    gram_mine = scatter_sum(gram_rows.reshape(frame_count, -1, rank), "frame")
    gram_rows = gather(gram_mine, "frame", frame_count).reshape(width, rank)
    gram = feat_gather(gram_rows)

    orthobasis = to_basis(sketch, gram)
    partial = lax.dot_general(
        trajectory, orthobasis, (((0,), (0,)), ((), ())), preferred_element_type=jnp.float32
    )
    summed = scatter_sum(partial.astype(jnp.bfloat16).reshape(frame_count, -1, rank), "frame")
    features_mine = (summed / math.sqrt(frames_all)).astype(jnp.bfloat16)

    by_rows = features_mine.T.reshape(frame_count, rank // frame_count, -1)
    swapped = lax.all_to_all(by_rows, "frame", 0, 0)
    projected = swapped.transpose(1, 0, 2).reshape(rank // frame_count, local_feats)

    partial_gram = lax.dot_general(
        features_mine, features_mine, (((0,), (0,)), ((), ())), preferred_element_type=jnp.float32
    )
    gram_mine = scatter_sum(
        partial_gram.astype(jnp.bfloat16).reshape(frame_count, -1, rank), "frame"
    )
    small_gram = jnp.sum(gather(gram_mine, "feat", feat_count), axis=0) / features_all
    return (orthobasis, projected, small_gram)


def solution(mesh):
    return jax.shard_map(
        per_device,
        mesh=mesh,
        in_specs=(P("frame", "feat"), P("feat", None)),
        out_specs=(P("frame", None), P("frame", "feat"), P("frame", None)),
        check_vma=False,
    )
```

```python
import math

import jax
import jax.numpy as jnp
from jax import lax
from jax.experimental import pallas as pl
from jax.experimental.pallas import tpu as pltpu
from jax.sharding import PartitionSpec as P

SUB, LANE = 8, 128
HI = lax.Precision.HIGHEST

def over_lanes(tile, column):
    return jnp.broadcast_to(tile[:, column:column + 1], (SUB, LANE))

def over_sublanes(tile, row):
    return jnp.broadcast_to(tile[row:row + 1, :], (SUB, LANE))

def invert_block(tiles):
    sub = lax.broadcasted_iota(jnp.int32, (SUB, LANE), 0)
    lane = lax.broadcasted_iota(jnp.int32, (SUB, LANE), 1)
    tiles = list(tiles)
    done = []
    count = len(tiles)
    for g in range(count):
        first = SUB * g
        in_panel = (lane >= first) & (lane < first + SUB)
        rows = tiles[g]
        columns = [over_lanes(rows, first + t) for t in range(SUB)]
        panel = jnp.where(in_panel, (lane - first == sub).astype(jnp.float32), rows)
        scale = jnp.ones((SUB, LANE), jnp.float32)
        inverse, coupling, pivot_rows = [], [], []
        for t in range(SUB):
            pivot = over_sublanes(columns[t], t)
            inv = 1.0 / pivot
            inverse.append(inv)
            pivot_rows.append(over_sublanes(panel, t))
            scale = jnp.where(sub == t, lax.rsqrt(pivot), scale)
            factor = jnp.where(sub > t, columns[t] * inv, 0.0)
            couple = {}
            for u in range(t + 1, SUB):
                couple[u] = over_sublanes(columns[u], t)
                columns[u] = columns[u] - factor * couple[u]
            coupling.append(couple)
            panel = panel - factor * pivot_rows[t]
        done.append(panel * scale)
        for i in range(g + 1, count):
            cols = [over_lanes(tiles[i], first + t) for t in range(SUB)]
            row = jnp.where(in_panel, 0.0, tiles[i])
            for t in range(SUB):
                f = cols[t] * inverse[t]
                for u in range(t + 1, SUB):
                    cols[u] = cols[u] - f * coupling[t][u]
                row = row - f * pivot_rows[t]
            tiles[i] = row
    return [jnp.where(lane <= sub + SUB * g, tile, 0.0) for g, tile in enumerate(done)]

def mm(a, b, dims):
    return lax.dot_general(a, b, (dims, ((), ())), precision=HI, preferred_element_type=jnp.float32)

def kernel(gram_ref, out_ref, aug):
    n = gram_ref.shape[0]
    blocks = n // LANE
    aug[:, :n] = gram_ref[...]
    aug[:, n:] = jnp.zeros((n, n), jnp.float32)
    out_ref[...] = jnp.zeros_like(out_ref)
    def step(k, _):
        at = pl.multiple_of(k * LANE, LANE)
        tiles = [aug[pl.ds(at + SUB * g, SUB), pl.ds(at, LANE)] for g in range(LANE // SUB)]
        inv = invert_block(tiles)
        for g, t in enumerate(inv):
            out_ref[pl.ds(at + SUB * g, SUB), pl.ds(at, LANE)] = t
        return _
    for k in range(blocks):
        lo, hi = k * LANE, (k + 1) * LANE
        step(k, 0)
        inv = out_ref[lo:hi, lo:hi]
        if k:
            out_ref[lo:hi, :lo] = mm(inv, aug[lo:hi, n:n + lo], ((1,), (0,)))
        if k + 1 < blocks:
            right = mm(inv, aug[lo:hi, hi:n], ((1,), (0,)))
            aug[hi:, hi:n] -= mm(right, right, ((0,), (0,)))
            aug[hi:, n:n + hi] -= mm(right, out_ref[lo:hi, :hi], ((0,), (0,)))

def inverse_factor(gram):
    n = gram.shape[0]
    return pl.pallas_call(
        kernel,
        out_shape=jax.ShapeDtypeStruct((n, n), jnp.float32),
        scratch_shapes=[pltpu.VMEM((n, 2 * n), jnp.float32)],
        compiler_params=pltpu.CompilerParams(vmem_limit_bytes=32 << 20),
    )(gram)


def lines(axis_size, stride):
    return [list(range(s, axis_size, stride)) for s in range(stride)]


def scatter_sum(blocks, axis, groups=None):
    got = lax.all_to_all(blocks, axis, 0, 0, axis_index_groups=groups)
    return jnp.sum(got.astype(jnp.float32), axis=0)


def gather(block, axis, count, groups=None):
    copies = jnp.broadcast_to(block, (count,) + block.shape)
    return lax.all_to_all(copies, axis, 0, 0, axis_index_groups=groups)


def swap_cores(block):
    count = lax.axis_size("feat")
    return lax.ppermute(block, "feat", [(i, i ^ 1) for i in range(count)])


def feat_scatter_sum(whole):
    count = lax.axis_size("feat")
    core = lax.axis_index("feat") % 2
    rows, columns = whole.shape
    halves = whole.reshape(2, rows // 2, columns)
    keep = lax.dynamic_index_in_dim(halves, core, 0, keepdims=False)
    give = lax.dynamic_index_in_dim(halves, 1 - core, 0, keepdims=False)
    half = keep + swap_cores(give)
    return scatter_sum(half.reshape(count // 2, -1, columns), "feat", lines(count, 2))


def feat_gather(block):
    count = lax.axis_size("feat")
    core = lax.axis_index("feat") % 2
    half = gather(block, "feat", count // 2, lines(count, 2)).reshape(-1, block.shape[1])
    other = swap_cores(half)
    low = jnp.where(core == 0, half, other)
    high = jnp.where(core == 0, other, half)
    return jnp.concatenate([low, high], axis=0)


def to_basis(sketch, gram):
    solved = mm(sketch, inverse_factor(gram), ((1,), (1,)))
    return solved.astype(jnp.bfloat16)


def per_device(trajectory, test_matrix):
    frame_count = lax.axis_size("frame")
    feat_count = lax.axis_size("feat")
    local_rows, local_feats = trajectory.shape
    frames_all = local_rows * frame_count
    features_all = local_feats * feat_count
    rank = test_matrix.shape[1]

    partial_sketch = jnp.dot(trajectory, test_matrix, preferred_element_type=jnp.float32)
    sketch = feat_gather(feat_scatter_sum(partial_sketch))

    width = rank // feat_count
    place = lax.axis_index("feat") % 2 * (feat_count // 2) + lax.axis_index("feat") // 2
    columns = lax.dynamic_slice_in_dim(sketch, place * width, width, axis=1)
    gram_rows = jnp.dot(columns.T, sketch, precision=lax.Precision.HIGHEST) / frames_all
    gram_mine = scatter_sum(gram_rows.reshape(frame_count, -1, rank), "frame")
    gram_rows = gather(gram_mine, "frame", frame_count).reshape(width, rank)
    gram = feat_gather(gram_rows)

    orthobasis = to_basis(sketch, gram)
    partial = lax.dot_general(
        trajectory, orthobasis, (((0,), (0,)), ((), ())), preferred_element_type=jnp.float32
    )
    summed = scatter_sum(partial.astype(jnp.bfloat16).reshape(frame_count, -1, rank), "frame")
    features_mine = (summed / math.sqrt(frames_all)).astype(jnp.bfloat16)

    by_rows = features_mine.T.reshape(frame_count, rank // frame_count, -1)
    swapped = lax.all_to_all(by_rows, "frame", 0, 0)
    projected = swapped.transpose(1, 0, 2).reshape(rank // frame_count, local_feats)

    partial_gram = lax.dot_general(
        features_mine, features_mine, (((0,), (0,)), ((), ())), preferred_element_type=jnp.float32
    )
    gram_mine = scatter_sum(
        partial_gram.astype(jnp.bfloat16).reshape(frame_count, -1, rank), "frame"
    )
    small_gram = jnp.sum(gather(gram_mine, "feat", feat_count), axis=0) / features_all
    return (orthobasis, projected, small_gram)


def solution(mesh):
    return jax.shard_map(
        per_device,
        mesh=mesh,
        in_specs=(P("frame", "feat"), P("feat", None)),
        out_specs=(P("frame", None), P("frame", "feat"), P("frame", None)),
        check_vma=False,
    )
```

```python
import functools
import math

import jax
import jax.numpy as jnp
from jax import lax
from jax.experimental import pallas as pl
from jax.experimental.pallas import tpu as pltpu
from jax.sharding import PartitionSpec as P

SUB, LANE = 8, 128
HI = lax.Precision.HIGHEST

def over_lanes(tile, column):
    return jnp.broadcast_to(tile[:, column:column + 1], (SUB, LANE))

def over_sublanes(tile, row):
    return jnp.broadcast_to(tile[row:row + 1, :], (SUB, LANE))

def invert_block(tiles):
    sub = lax.broadcasted_iota(jnp.int32, (SUB, LANE), 0)
    lane = lax.broadcasted_iota(jnp.int32, (SUB, LANE), 1)
    tiles = list(tiles)
    done = []
    count = len(tiles)
    for g in range(count):
        first = SUB * g
        in_panel = (lane >= first) & (lane < first + SUB)
        rows = tiles[g]
        columns = [over_lanes(rows, first + t) for t in range(SUB)]
        panel = jnp.where(in_panel, (lane - first == sub).astype(jnp.float32), rows)
        scale = jnp.ones((SUB, LANE), jnp.float32)
        inverse, coupling, pivot_rows = [], [], []
        for t in range(SUB):
            pivot = over_sublanes(columns[t], t)
            inv = 1.0 / pivot
            inverse.append(inv)
            pivot_rows.append(over_sublanes(panel, t))
            scale = jnp.where(sub == t, lax.rsqrt(pivot), scale)
            factor = jnp.where(sub > t, columns[t] * inv, 0.0)
            couple = {}
            for u in range(t + 1, SUB):
                couple[u] = over_sublanes(columns[u], t)
                columns[u] = columns[u] - factor * couple[u]
            coupling.append(couple)
            panel = panel - factor * pivot_rows[t]
        done.append(panel * scale)
        for i in range(g + 1, count):
            cols = [over_lanes(tiles[i], first + t) for t in range(SUB)]
            row = jnp.where(in_panel, 0.0, tiles[i])
            for t in range(SUB):
                f = cols[t] * inverse[t]
                for u in range(t + 1, SUB):
                    cols[u] = cols[u] - f * coupling[t][u]
                row = row - f * pivot_rows[t]
            tiles[i] = row
    return [jnp.where(lane <= sub + SUB * g, tile, 0.0) for g, tile in enumerate(done)]

def mm(a, b, dims):
    return lax.dot_general(a, b, (dims, ((), ())), precision=HI, preferred_element_type=jnp.float32)

def kernel(gram_ref, out_ref, aug):
    n = gram_ref.shape[0]
    blocks = n // LANE
    aug[:, :n] = gram_ref[...]
    aug[:, n:] = jnp.zeros((n, n), jnp.float32)
    out_ref[...] = jnp.zeros_like(out_ref)
    def step(k, _):
        at = pl.multiple_of(k * LANE, LANE)
        tiles = [aug[pl.ds(at + SUB * g, SUB), pl.ds(at, LANE)] for g in range(LANE // SUB)]
        inv = invert_block(tiles)
        for g, t in enumerate(inv):
            out_ref[pl.ds(at + SUB * g, SUB), pl.ds(at, LANE)] = t
        return _
    for k in range(blocks):
        lo, hi = k * LANE, (k + 1) * LANE
        step(k, 0)
        inv = out_ref[lo:hi, lo:hi]
        if k:
            out_ref[lo:hi, :lo] = mm(inv, aug[lo:hi, n:n + lo], ((1,), (0,)))
        if k + 1 < blocks:
            right = mm(inv, aug[lo:hi, hi:n], ((1,), (0,)))
            aug[hi:, hi:n] -= mm(right, right, ((0,), (0,)))
            aug[hi:, n:n + hi] -= mm(right, out_ref[lo:hi, :hi], ((0,), (0,)))

def inverse_factor(gram):
    n = gram.shape[0]
    return pl.pallas_call(
        kernel,
        out_shape=jax.ShapeDtypeStruct((n, n), jnp.float32),
        scratch_shapes=[pltpu.VMEM((n, 2 * n), jnp.float32)],
        compiler_params=pltpu.CompilerParams(vmem_limit_bytes=32 << 20),
    )(gram)


def lines(axis_size, stride):
    return [list(range(s, axis_size, stride)) for s in range(stride)]


def scatter_sum(blocks, axis, groups=None):
    got = lax.all_to_all(blocks, axis, 0, 0, axis_index_groups=groups)
    return jnp.sum(got.astype(jnp.float32), axis=0)


def gather(block, axis, count, groups=None):
    copies = jnp.broadcast_to(block, (count,) + block.shape)
    return lax.all_to_all(copies, axis, 0, 0, axis_index_groups=groups)


def swap_cores(block):
    count = lax.axis_size("feat")
    return lax.ppermute(block, "feat", [(i, i ^ 1) for i in range(count)])


def feat_scatter_sum(whole):
    count = lax.axis_size("feat")
    core = lax.axis_index("feat") % 2
    rows, columns = whole.shape
    halves = whole.reshape(2, rows // 2, columns)
    keep = lax.dynamic_index_in_dim(halves, core, 0, keepdims=False)
    give = lax.dynamic_index_in_dim(halves, 1 - core, 0, keepdims=False)
    half = keep + swap_cores(give)
    return scatter_sum(half.reshape(count // 2, -1, columns), "feat", lines(count, 2))


def feat_gather(block):
    count = lax.axis_size("feat")
    core = lax.axis_index("feat") % 2
    half = gather(block, "feat", count // 2, lines(count, 2)).reshape(-1, block.shape[1])
    other = swap_cores(half)
    low = jnp.where(core == 0, half, other)
    high = jnp.where(core == 0, other, half)
    return jnp.concatenate([low, high], axis=0)


def tail_kernel(scale, summed_ref, inverse_ref, out_ref, wide):
    mine, n = summed_ref.shape
    wide[...] = jnp.zeros_like(wide)
    wide[:mine, :] = summed_ref[...]
    projected = (mm(inverse_ref[...], wide[...], ((1,), (1,))) * scale).astype(jnp.bfloat16)
    out_ref[:, n:] = projected
    out_ref[:, :n] = lax.dot_general(
        projected, projected, (((1,), (1,)), ((), ())), preferred_element_type=jnp.float32
    ).astype(jnp.bfloat16)


def project(summed, inverse, scale):
    n = inverse.shape[0]
    return pl.pallas_call(
        functools.partial(tail_kernel, scale),
        out_shape=jax.ShapeDtypeStruct((n, n + LANE), jnp.bfloat16),
        scratch_shapes=[pltpu.VMEM((LANE, n), jnp.float32)],
        compiler_params=pltpu.CompilerParams(vmem_limit_bytes=32 << 20),
    )(summed, inverse)


def per_device(trajectory, test_matrix):
    frame_count = lax.axis_size("frame")
    feat_count = lax.axis_size("feat")
    local_rows, local_feats = trajectory.shape
    frames_all = local_rows * frame_count
    features_all = local_feats * feat_count
    rank = test_matrix.shape[1]

    partial_sketch = jnp.dot(trajectory, test_matrix, preferred_element_type=jnp.float32)
    by_feature = lax.optimization_barrier(trajectory.T)
    sketch = feat_gather(feat_scatter_sum(partial_sketch))

    width = rank // feat_count
    place = lax.axis_index("feat") % 2 * (feat_count // 2) + lax.axis_index("feat") // 2
    columns = lax.dynamic_slice_in_dim(sketch, place * width, width, axis=1)
    gram_rows = jnp.dot(columns.T, sketch, precision=lax.Precision.HIGHEST) / frames_all

    high = sketch.astype(jnp.bfloat16)
    low = (sketch - high.astype(jnp.float32)).astype(jnp.bfloat16)
    partial = jnp.dot(by_feature, high, preferred_element_type=jnp.float32) + jnp.dot(
        by_feature, low, preferred_element_type=jnp.float32
    )
    x_count = 4
    z_count = frame_count // x_count
    x_groups = [list(range(s, s + x_count)) for s in range(0, frame_count, x_count)]
    some = lax.psum_scatter(
        partial, "frame", scatter_dimension=0, axis_index_groups=x_groups, tiled=True
    )
    summed = lax.psum_scatter(
        some, "frame", scatter_dimension=0, axis_index_groups=lines(frame_count, x_count), tiled=True
    )

    gram_mine = scatter_sum(gram_rows.reshape(frame_count, -1, rank), "frame")
    gram_rows = gather(gram_mine, "frame", frame_count).reshape(width, rank)
    inverse = inverse_factor(feat_gather(gram_rows))

    orthobasis = mm(sketch, inverse, ((1,), (1,))).astype(jnp.bfloat16)
    parts = project(summed, inverse, 1.0 / math.sqrt(frames_all))
    got = lax.all_to_all(parts.reshape(frame_count, -1, rank + LANE), "frame", 0, 0)
    gram_mine = jnp.sum(got[:, :, :rank].astype(jnp.float32), axis=0).astype(jnp.bfloat16)
    small_gram = jnp.sum(gather(gram_mine, "feat", feat_count).astype(jnp.float32), axis=0) / features_all

    columns = got[:, :, rank : rank + local_feats // frame_count]
    columns = columns.reshape(z_count, x_count, rank // frame_count, -1)
    projected = columns.transpose(2, 1, 0, 3).reshape(rank // frame_count, local_feats)
    return (orthobasis, projected, small_gram)


def solution(mesh):
    return jax.shard_map(
        per_device,
        mesh=mesh,
        in_specs=(P("frame", "feat"), P("feat", None)),
        out_specs=(P("frame", None), P("frame", "feat"), P("frame", None)),
        check_vma=False,
    )
```

```python
import functools
import math

import jax
import jax.numpy as jnp
from jax import lax
from jax.experimental import pallas as pl
from jax.experimental.pallas import tpu as pltpu
from jax.sharding import PartitionSpec as P

SUB, LANE = 8, 128
HI = lax.Precision.HIGHEST

def over_lanes(tile, column):
    return jnp.broadcast_to(tile[:, column:column + 1], (SUB, LANE))

def over_sublanes(tile, row):
    return jnp.broadcast_to(tile[row:row + 1, :], (SUB, LANE))

def invert_block(tiles):
    sub = lax.broadcasted_iota(jnp.int32, (SUB, LANE), 0)
    lane = lax.broadcasted_iota(jnp.int32, (SUB, LANE), 1)
    tiles = list(tiles)
    done = []
    count = len(tiles)
    for g in range(count):
        first = SUB * g
        in_panel = (lane >= first) & (lane < first + SUB)
        rows = tiles[g]
        columns = [over_lanes(rows, first + t) for t in range(SUB)]
        panel = jnp.where(in_panel, (lane - first == sub).astype(jnp.float32), rows)
        scale = jnp.ones((SUB, LANE), jnp.float32)
        inverse, coupling, pivot_rows = [], [], []
        for t in range(SUB):
            pivot = over_sublanes(columns[t], t)
            inv = 1.0 / pivot
            inverse.append(inv)
            pivot_rows.append(over_sublanes(panel, t))
            scale = jnp.where(sub == t, lax.rsqrt(pivot), scale)
            factor = jnp.where(sub > t, columns[t] * inv, 0.0)
            couple = {}
            for u in range(t + 1, SUB):
                couple[u] = over_sublanes(columns[u], t)
                columns[u] = columns[u] - factor * couple[u]
            coupling.append(couple)
            panel = panel - factor * pivot_rows[t]
        done.append(panel * scale)
        for i in range(g + 1, count):
            cols = [over_lanes(tiles[i], first + t) for t in range(SUB)]
            row = jnp.where(in_panel, 0.0, tiles[i])
            for t in range(SUB):
                f = cols[t] * inverse[t]
                for u in range(t + 1, SUB):
                    cols[u] = cols[u] - f * coupling[t][u]
                row = row - f * pivot_rows[t]
            tiles[i] = row
    return [jnp.where(lane <= sub + SUB * g, tile, 0.0) for g, tile in enumerate(done)]

def mm(a, b, dims):
    return lax.dot_general(a, b, (dims, ((), ())), precision=HI, preferred_element_type=jnp.float32)

PACKED = ((0, 0), (0, 1), (0, 2), (2, 2), (2, 3))


def gram_kernel(core_ref, half_ref, other_ref, _, out_ref):
    core = core_ref[0]

    def block(ref, i):
        return ref[:, pl.ds(pl.multiple_of((i + core) % 4 * LANE, LANE), LANE)]

    total = jnp.zeros((LANE, len(PACKED) * LANE), jnp.float32)
    for ref in (half_ref, other_ref):
        parts = [block(ref, i) for i in range(4)]
        first = mm(parts[0], jnp.concatenate(parts[:3], axis=1), ((0,), (0,)))
        second = mm(parts[2], jnp.concatenate(parts[2:], axis=1), ((0,), (0,)))
        total = total + jnp.concatenate([first, second], axis=1)
    out_ref[...] = total


def gram_blocks(core, half, other, after):
    return pl.pallas_call(
        gram_kernel,
        in_specs=[pl.BlockSpec(memory_space=pltpu.SMEM)]
        + [pl.BlockSpec(memory_space=pltpu.VMEM)] * 2
        + [pl.BlockSpec(memory_space=pl.ANY)],
        out_shape=jax.ShapeDtypeStruct((LANE, len(PACKED) * LANE), jnp.float32),
        compiler_params=pltpu.CompilerParams(vmem_limit_bytes=32 << 20),
    )(core, half, other, after)


def factor_kernel(core_ref, mine_ref, other_ref, out_ref, aug):
    n = out_ref.shape[0]
    blocks = n // LANE
    core = core_ref[0]
    aug[...] = jnp.zeros_like(aug)
    out_ref[...] = jnp.zeros_like(out_ref)
    for at, (i, j) in enumerate(PACKED):
        columns = slice(at * LANE, (at + 1) * LANE)
        mine, other = mine_ref[:, columns], other_ref[:, columns]
        for c in range(2):
            value = jnp.where(core == c, mine, other)
            row, column = (i + c) % 4, (j + c) % 4
            if row > column:
                row, column, value = column, row, value.T
            aug[row * LANE : (row + 1) * LANE, column * LANE : (column + 1) * LANE] = value
    for k in range(blocks):
        lo, hi = k * LANE, (k + 1) * LANE
        tiles = [aug[lo + SUB * g : lo + SUB * (g + 1), lo:hi] for g in range(LANE // SUB)]
        for g, tile in enumerate(invert_block(tiles)):
            out_ref[lo + SUB * g : lo + SUB * (g + 1), lo:hi] = tile
        inv = out_ref[lo:hi, lo:hi]
        if k:
            out_ref[lo:hi, :lo] = mm(inv, aug[lo:hi, n : n + lo], ((1,), (0,)))
        if k + 1 < blocks:
            right = mm(inv, aug[lo:hi, hi:n], ((1,), (0,)))
            aug[hi:, hi:n] -= mm(right, right, ((0,), (0,)))
            aug[hi:, n : n + hi] -= mm(right, out_ref[lo:hi, :hi], ((0,), (0,)))


def inverse_factor(core, mine, other):
    n = 4 * LANE
    return pl.pallas_call(
        factor_kernel,
        in_specs=[pl.BlockSpec(memory_space=pltpu.SMEM)] + [pl.BlockSpec(memory_space=pltpu.VMEM)] * 2,
        out_shape=jax.ShapeDtypeStruct((n, n), jnp.float32),
        scratch_shapes=[pltpu.VMEM((n, 2 * n), jnp.float32)],
        compiler_params=pltpu.CompilerParams(vmem_limit_bytes=32 << 20),
        cost_estimate=pl.CostEstimate(
            flops=20_000_000_000, bytes_accessed=8 * n * n, transcendentals=n
        ),
    )(core, mine, other)


def lines(axis_size, stride):
    return [list(range(s, axis_size, stride)) for s in range(stride)]


def scatter_sum(blocks, axis, groups=None):
    got = lax.all_to_all(blocks, axis, 0, 0, axis_index_groups=groups)
    return jnp.sum(got.astype(jnp.float32), axis=0)


def gather(block, axis, count, groups=None):
    copies = jnp.broadcast_to(block, (count,) + block.shape)
    return lax.all_to_all(copies, axis, 0, 0, axis_index_groups=groups)


def swap_cores(block):
    count = lax.axis_size("feat")
    return lax.ppermute(block, "feat", [(i, i ^ 1) for i in range(count)])


def feat_scatter_sum(whole):
    count = lax.axis_size("feat")
    core = lax.axis_index("feat") % 2
    rows, columns = whole.shape
    halves = whole.reshape(2, rows // 2, columns)
    keep = lax.dynamic_index_in_dim(halves, core, 0, keepdims=False)
    give = lax.dynamic_index_in_dim(halves, 1 - core, 0, keepdims=False)
    half = keep + swap_cores(give)
    return scatter_sum(half.reshape(count // 2, -1, columns), "feat", lines(count, 2))


def feat_gather(block):
    count = lax.axis_size("feat")
    half = gather(block, "feat", count // 2, lines(count, 2)).reshape(-1, block.shape[1])
    return half, swap_cores(half)


def tail_kernel(scale, summed_ref, inverse_ref, out_ref, wide):
    mine, n = summed_ref.shape
    wide[...] = jnp.zeros_like(wide)
    wide[:mine, :] = summed_ref[...]
    projected = (mm(inverse_ref[...], wide[...], ((1,), (1,))) * scale).astype(jnp.bfloat16)
    out_ref[:, n:] = projected
    out_ref[:, :n] = lax.dot_general(
        projected, projected, (((1,), (1,)), ((), ())), preferred_element_type=jnp.float32
    ).astype(jnp.bfloat16)


def project(summed, inverse, scale):
    n = inverse.shape[0]
    return pl.pallas_call(
        functools.partial(tail_kernel, scale),
        out_shape=jax.ShapeDtypeStruct((n, n + LANE), jnp.bfloat16),
        scratch_shapes=[pltpu.VMEM((LANE, n), jnp.float32)],
        compiler_params=pltpu.CompilerParams(vmem_limit_bytes=32 << 20),
    )(summed, inverse)


def per_device(trajectory, test_matrix):
    frame_count = lax.axis_size("frame")
    feat_count = lax.axis_size("feat")
    local_rows, local_feats = trajectory.shape
    frames_all = local_rows * frame_count
    features_all = local_feats * feat_count
    rank = test_matrix.shape[1]

    partial_sketch = jnp.dot(trajectory, test_matrix, preferred_element_type=jnp.float32)
    half, other = feat_gather(feat_scatter_sum(partial_sketch))
    core = lax.axis_index("feat") % 2
    core_word = core.astype(jnp.int32).reshape(1)
    sketch = jnp.concatenate(
        [jnp.where(core == 0, half, other), jnp.where(core == 0, other, half)], axis=0
    )

    high = sketch.astype(jnp.bfloat16)
    low = (sketch - high.astype(jnp.float32)).astype(jnp.bfloat16)
    partial = jnp.dot(trajectory.T, high, preferred_element_type=jnp.float32) + jnp.dot(
        trajectory.T, low, preferred_element_type=jnp.float32
    )
    x_count = 4
    z_count = frame_count // x_count
    x_groups = [list(range(s, s + x_count)) for s in range(0, frame_count, x_count)]
    some = lax.psum_scatter(
        partial, "frame", scatter_dimension=0, axis_index_groups=x_groups, tiled=True
    )
    summed = scatter_sum(some.reshape(z_count, -1, rank), "frame", lines(frame_count, x_count))

    packed = gram_blocks(core_word, half, other, partial)
    packed = scatter_sum(packed.reshape(frame_count, -1, packed.shape[1]), "frame") / frames_all
    packed = gather(packed, "frame", frame_count).reshape(LANE, -1)
    inverse = inverse_factor(core_word, packed, swap_cores(packed))

    orthobasis = mm(sketch, inverse, ((1,), (1,))).astype(jnp.bfloat16)
    parts = project(summed, inverse, 1.0 / math.sqrt(frames_all))
    got = lax.all_to_all(parts.reshape(frame_count, -1, rank + LANE), "frame", 0, 0)
    gram_mine = jnp.sum(got[:, :, :rank].astype(jnp.float32), axis=0).astype(jnp.bfloat16)
    small_gram = jnp.sum(gather(gram_mine, "feat", feat_count).astype(jnp.float32), axis=0) / features_all

    columns = got[:, :, rank : rank + local_feats // frame_count]
    columns = columns.reshape(z_count, x_count, rank // frame_count, -1)
    projected = columns.transpose(2, 1, 0, 3).reshape(rank // frame_count, local_feats)
    return (orthobasis, projected, small_gram)


def solution(mesh):
    return jax.shard_map(
        per_device,
        mesh=mesh,
        in_specs=(P("frame", "feat"), P("feat", None)),
        out_specs=(P("frame", None), P("frame", "feat"), P("frame", None)),
        check_vma=False,
    )
```

```python
import functools
import math

import jax
import jax.numpy as jnp
from jax import lax
from jax.experimental import pallas as pl
from jax.experimental.pallas import tpu as pltpu
from jax.sharding import PartitionSpec as P

SUB, LANE = 8, 128
HI = lax.Precision.HIGHEST

def over_lanes(tile, column):
    return jnp.broadcast_to(tile[:, column:column + 1], (SUB, LANE))

def over_sublanes(tile, row):
    return jnp.broadcast_to(tile[row:row + 1, :], (SUB, LANE))

def invert_block(tiles):
    sub = lax.broadcasted_iota(jnp.int32, (SUB, LANE), 0)
    lane = lax.broadcasted_iota(jnp.int32, (SUB, LANE), 1)
    tiles = list(tiles)
    done = []
    count = len(tiles)
    for g in range(count):
        first = SUB * g
        in_panel = (lane >= first) & (lane < first + SUB)
        rows = tiles[g]
        columns = [over_lanes(rows, first + t) for t in range(SUB)]
        panel = jnp.where(in_panel, (lane - first == sub).astype(jnp.float32), rows)
        scale = jnp.ones((SUB, LANE), jnp.float32)
        inverse, coupling, pivot_rows = [], [], []
        for t in range(SUB):
            pivot = over_sublanes(columns[t], t)
            inv = 1.0 / pivot
            inverse.append(inv)
            pivot_rows.append(over_sublanes(panel, t))
            scale = jnp.where(sub == t, lax.rsqrt(pivot), scale)
            factor = jnp.where(sub > t, columns[t] * inv, 0.0)
            couple = {}
            for u in range(t + 1, SUB):
                couple[u] = over_sublanes(columns[u], t)
                columns[u] = columns[u] - factor * couple[u]
            coupling.append(couple)
            panel = panel - factor * pivot_rows[t]
        done.append(panel * scale)
        for i in range(g + 1, count):
            cols = [over_lanes(tiles[i], first + t) for t in range(SUB)]
            row = jnp.where(in_panel, 0.0, tiles[i])
            for t in range(SUB):
                f = cols[t] * inverse[t]
                for u in range(t + 1, SUB):
                    cols[u] = cols[u] - f * coupling[t][u]
                row = row - f * pivot_rows[t]
            tiles[i] = row
    return [jnp.where(lane <= sub + SUB * g, tile, 0.0) for g, tile in enumerate(done)]

def mm(a, b, dims):
    return lax.dot_general(a, b, (dims, ((), ())), precision=HI, preferred_element_type=jnp.float32)

PACKED = ((0, 0), (0, 1), (0, 2), (2, 2), (2, 3))


def gram_kernel(core_ref, half_ref, other_ref, *refs):
    out_ref = refs[-1]
    core = core_ref[0]

    def block(ref, i):
        return ref[:, pl.ds(pl.multiple_of((i + core) % 4 * LANE, LANE), LANE)]

    total = jnp.zeros((LANE, len(PACKED) * LANE), jnp.float32)
    for ref in (half_ref, other_ref):
        parts = [block(ref, i) for i in range(4)]
        first = mm(parts[0], jnp.concatenate(parts[:3], axis=1), ((0,), (0,)))
        second = mm(parts[2], jnp.concatenate(parts[2:], axis=1), ((0,), (0,)))
        total = total + jnp.concatenate([first, second], axis=1)
    out_ref[...] = total


def gram_blocks(core, half, other, after):
    return pl.pallas_call(
        gram_kernel,
        in_specs=[pl.BlockSpec(memory_space=pltpu.SMEM)]
        + [pl.BlockSpec(memory_space=pltpu.VMEM)] * 2
        + [pl.BlockSpec(memory_space=pl.ANY)] * len(after),
        out_shape=jax.ShapeDtypeStruct((LANE, len(PACKED) * LANE), jnp.float32),
        compiler_params=pltpu.CompilerParams(vmem_limit_bytes=32 << 20),
    )(core, half, other, *after)


def factor_kernel(core_ref, mine_ref, other_ref, _, out_ref, aug):
    n = out_ref.shape[0]
    blocks = n // LANE
    core = core_ref[0]
    aug[...] = jnp.zeros_like(aug)
    out_ref[...] = jnp.zeros_like(out_ref)
    for at, (i, j) in enumerate(PACKED):
        columns = slice(at * LANE, (at + 1) * LANE)
        mine, other = mine_ref[:, columns], other_ref[:, columns]
        for c in range(2):
            value = jnp.where(core == c, mine, other)
            row, column = (i + c) % 4, (j + c) % 4
            if row > column:
                row, column, value = column, row, value.T
            aug[row * LANE : (row + 1) * LANE, column * LANE : (column + 1) * LANE] = value
    for k in range(blocks):
        lo, hi = k * LANE, (k + 1) * LANE
        tiles = [aug[lo + SUB * g : lo + SUB * (g + 1), lo:hi] for g in range(LANE // SUB)]
        for g, tile in enumerate(invert_block(tiles)):
            out_ref[lo + SUB * g : lo + SUB * (g + 1), lo:hi] = tile
        inv = out_ref[lo:hi, lo:hi]
        if k:
            out_ref[lo:hi, :lo] = mm(inv, aug[lo:hi, n : n + lo], ((1,), (0,)))
        if k + 1 < blocks:
            right = mm(inv, aug[lo:hi, hi:n], ((1,), (0,)))
            aug[hi:, hi:n] -= mm(right, right, ((0,), (0,)))
            aug[hi:, n : n + hi] -= mm(right, out_ref[lo:hi, :hi], ((0,), (0,)))


def inverse_factor(core, mine, other, after):
    n = 4 * LANE
    return pl.pallas_call(
        factor_kernel,
        in_specs=[pl.BlockSpec(memory_space=pltpu.SMEM)]
        + [pl.BlockSpec(memory_space=pltpu.VMEM)] * 2
        + [pl.BlockSpec(memory_space=pl.ANY)],
        out_shape=jax.ShapeDtypeStruct((n, n), jnp.float32),
        scratch_shapes=[pltpu.VMEM((n, 2 * n), jnp.float32)],
        compiler_params=pltpu.CompilerParams(vmem_limit_bytes=32 << 20),
        cost_estimate=pl.CostEstimate(
            flops=20_000_000_000, bytes_accessed=8 * n * n, transcendentals=n
        ),
    )(core, mine, other, after)


def lines(axis_size, stride):
    return [list(range(s, axis_size, stride)) for s in range(stride)]


def scatter_sum(blocks, axis, groups=None):
    got = lax.all_to_all(blocks, axis, 0, 0, axis_index_groups=groups)
    return jnp.sum(got.astype(jnp.float32), axis=0)


def gather(block, axis, count, groups=None):
    copies = jnp.broadcast_to(block, (count,) + block.shape)
    return lax.all_to_all(copies, axis, 0, 0, axis_index_groups=groups)


def swap_cores(block):
    count = lax.axis_size("feat")
    return lax.ppermute(block, "feat", [(i, i ^ 1) for i in range(count)])


def feat_scatter_sum(whole):
    count = lax.axis_size("feat")
    core = lax.axis_index("feat") % 2
    rows, columns = whole.shape
    halves = whole.reshape(2, rows // 2, columns)
    keep = lax.dynamic_index_in_dim(halves, core, 0, keepdims=False)
    give = lax.dynamic_index_in_dim(halves, 1 - core, 0, keepdims=False)
    half = keep + swap_cores(give)
    return scatter_sum(half.reshape(count // 2, -1, columns), "feat", lines(count, 2))


def feat_gather(block):
    count = lax.axis_size("feat")
    half = gather(block, "feat", count // 2, lines(count, 2)).reshape(-1, block.shape[1])
    return half, swap_cores(half)


def tail_kernel(scale, core_ref, summed_ref, inverse_ref, give_ref, keep_ref, projected_ref, wide):
    mine, n = summed_ref.shape
    wide[...] = jnp.zeros_like(wide)
    wide[:mine, :] = summed_ref[...]
    projected = (mm(inverse_ref[...], wide[...], ((1,), (1,))) * scale).astype(jnp.bfloat16)
    projected_ref[...] = projected
    for ref, half in ((give_ref, 1 - core_ref[0]), (keep_ref, core_ref[0])):
        rows = projected_ref[pl.ds(pl.multiple_of(half * (n // 2), n // 2), n // 2), :]
        term = lax.dot_general(
            projected, rows, (((1,), (1,)), ((), ())), preferred_element_type=jnp.float32
        )
        ref[...] = term.astype(ref.dtype)


def project(core, summed, inverse, scale):
    n = inverse.shape[0]
    return pl.pallas_call(
        functools.partial(tail_kernel, scale),
        in_specs=[pl.BlockSpec(memory_space=pltpu.SMEM)] + [pl.BlockSpec(memory_space=pltpu.VMEM)] * 2,
        out_shape=[
            jax.ShapeDtypeStruct((n, n // 2), jnp.bfloat16),
            jax.ShapeDtypeStruct((n, n // 2), jnp.float32),
            jax.ShapeDtypeStruct((n, LANE), jnp.bfloat16),
        ],
        scratch_shapes=[pltpu.VMEM((LANE, n), jnp.float32)],
        compiler_params=pltpu.CompilerParams(vmem_limit_bytes=32 << 20),
    )(core, summed, inverse)


def per_device(trajectory, test_matrix):
    frame_count = lax.axis_size("frame")
    feat_count = lax.axis_size("feat")
    local_rows, local_feats = trajectory.shape
    frames_all = local_rows * frame_count
    features_all = local_feats * feat_count
    rank = test_matrix.shape[1]

    partial_sketch = jnp.dot(trajectory, test_matrix, preferred_element_type=jnp.float32)
    half, other = feat_gather(feat_scatter_sum(partial_sketch))
    core = lax.axis_index("feat") % 2
    core_word = core.astype(jnp.int32).reshape(1)
    sketch = jnp.concatenate(
        [jnp.where(core == 0, half, other), jnp.where(core == 0, other, half)], axis=0
    )

    high = sketch.astype(jnp.bfloat16)
    low = (sketch - high.astype(jnp.float32)).astype(jnp.bfloat16)
    x_count = 4
    z_count = frame_count // x_count
    x = lax.axis_index("frame") % x_count

    def product(piece):
        size = local_feats // x_count
        columns = lax.dynamic_slice_in_dim(trajectory, piece * size, size, axis=1)
        return jnp.dot(columns.T, high, preferred_element_type=jnp.float32) + jnp.dot(
            columns.T, low, preferred_element_type=jnp.float32
        )

    some, sent = [], []
    for step in (2, 1, 3):
        to = [(i, i // x_count * x_count + (i + step) % x_count) for i in range(frame_count)]
        sent.append(product((x + step) % x_count))
        some.append(lax.ppermute(sent[-1], "frame", to))
    own = product(x)
    some = (own + some[0]) + (some[1] + some[2])
    summed = scatter_sum(some.reshape(z_count, -1, rank), "frame", lines(frame_count, x_count))

    packed = gram_blocks(core_word, half, other, sent)
    packed = scatter_sum(packed.reshape(frame_count, -1, packed.shape[1]), "frame") / frames_all
    packed = gather(packed, "frame", frame_count).reshape(LANE, -1)
    inverse = inverse_factor(core_word, packed, swap_cores(packed), some)

    orthobasis = mm(sketch, inverse, ((1,), (1,))).astype(jnp.bfloat16)
    give, keep, columns = project(core_word, summed, inverse, 1.0 / math.sqrt(frames_all))
    term = (keep + swap_cores(give).astype(jnp.float32)).astype(jnp.bfloat16)
    parts = jnp.concatenate([term, columns], axis=1).reshape(frame_count, -1, rank // 2 + LANE)
    got = lax.all_to_all(parts, "frame", 0, 0)
    term = jnp.sum(got[:, :, : rank // 2].astype(jnp.float32), axis=0).astype(jnp.bfloat16)
    terms = gather(term, "feat", feat_count // 2, lines(feat_count, 2))
    mine = jnp.sum(terms.astype(jnp.float32), axis=0) / features_all
    theirs = swap_cores(mine)
    small_gram = jnp.concatenate(
        [jnp.where(core == 0, mine, theirs), jnp.where(core == 0, theirs, mine)], axis=1
    )

    columns = got[:, :, rank // 2 : rank // 2 + local_feats // frame_count]
    columns = columns.reshape(z_count, x_count, rank // frame_count, -1)
    projected = columns.transpose(2, 1, 0, 3).reshape(rank // frame_count, local_feats)
    return (orthobasis, projected, small_gram)


def solution(mesh):
    return jax.shard_map(
        per_device,
        mesh=mesh,
        in_specs=(P("frame", "feat"), P("feat", None)),
        out_specs=(P("frame", None), P("frame", "feat"), P("frame", None)),
        check_vma=False,
    )
```
